32 devices in a mesh: groups: 2 (over x), blk: 16 (over z, y, core).
Axes of the slice: x: 2, y: 2, z: 4, core: 2. Of those that a mesh axis runs over, the one named last changes fastest.
Arguments:
- embeddings: bfloat16 [16384, 768], P(('groups', 'blk')), parts along dimension 0
- doc_order: int32 [16384], P(('groups', 'blk')), parts along dimension 0, may hold values from 0 to 8191, each once
- neighbours: int32 [32, 4], P('groups'), parts along dimension 0, may hold values from 0 to 15, as said below
Outputs:
- earlier_max: float32 [16384], P(('groups', 'blk')), parts along dimension 0
- later_max: bfloat16 [16384], P(('groups', 'blk')), parts along dimension 0
The draws below stay inside these ranges and needn't reach their ends.
There are 2 independent parts, one for each index of `groups`. The reference program is written for one: setup_inputs(seed, part) draws one part's arguments, and reference() takes and returns one part's arrays. A program takes and returns all parts, laid end to end along the dimension named above; each array names one. Nothing has to cross between parts.
Inputs may be any that keep to these rules, and one draw needn't show every extreme that they name: Every entry of neighbours[b] is a block at distance at most 2 from b along the loop of 16 blocks, (b + k) mod 16 with -2 <= k <= 2; block 0 lists both blocks at distance 2; a block may list an entry several times or list itself.
All inputs are finite; a program needn't handle non-finite values.
Results may differ from the reference program's by a relative error of at most 0.0028.
Values may be sent and summed in bfloat16 or wider, within the bound.
A program may use at most 64 MiB of HBM per device.

```python
import math
import jax
import jax.numpy as jnp
from jax import lax

D = 768
ROWS_DEV = 512
REACH = 2
SLOTS = 4
BLOCKS = 16
DOCS = 8192
TOPICS_BLK = 128


def draw_embeddings(key, part):
    keys = jax.random.split(key, 5)
    positions = jnp.arange(DOCS, dtype=jnp.int32)
    home_block = positions // ROWS_DEV
    moved = jax.random.randint(keys[0], (DOCS,), -REACH, REACH + 1)
    picked = jax.random.randint(keys[1], (DOCS,), 0, TOPICS_BLK)
    topic = (home_block + moved) % BLOCKS * TOPICS_BLK + picked
    topic_vectors = jax.vmap(lambda t: jax.random.normal(jax.random.fold_in(keys[2], t), (D,), jnp.float32))(topic)
    strength = jnp.exp(jax.random.uniform(keys[3], (DOCS, 1), jnp.float32, math.log(0.5), math.log(3.0)))
    noise = jax.random.normal(keys[4], (DOCS, D), jnp.float32)
    return (strength * topic_vectors + noise).astype(jnp.bfloat16)


def draw_neighbours(key, part):
    keys = jax.random.split(key, 2)
    moved = jax.random.randint(keys[0], (BLOCKS, SLOTS), -REACH, REACH + 1)
    moved = moved * jax.random.randint(keys[1], (BLOCKS, SLOTS), 0, 2)
    listed = (jnp.arange(BLOCKS, dtype=jnp.int32)[:, None] + moved) % BLOCKS
    listed = listed.at[0, 0].set(REACH % BLOCKS)
    listed = listed.at[0, 1].set((BLOCKS - REACH) % BLOCKS)
    return listed.astype(jnp.int32)


def setup_inputs(seed: int = 0, part: int = 0) -> dict:
    splits = jax.random.split(jax.random.key(seed), 4)
    part_splits = jax.random.split(jax.random.fold_in(splits[3], part), 4)
    embeddings = draw_embeddings(jax.random.fold_in(jax.random.fold_in(splits[3], part), 71), part)
    doc_order = jax.random.permutation(part_splits[1], DOCS).astype(jnp.int32)
    neighbours = draw_neighbours(jax.random.fold_in(jax.random.fold_in(splits[3], part), 71), part)
    return dict(embeddings=embeddings, doc_order=doc_order, neighbours=neighbours)


def normalize(embeddings):
    values = embeddings.astype(jnp.float32)
    inverse = lax.rsqrt(lax.optimization_barrier(jnp.sum(values * values, axis=-1, keepdims=True)) + 1e-06)
    return (values * inverse).astype(jnp.bfloat16)

def reference(embeddings, doc_order, neighbours):
    units = normalize(embeddings)
    unit_blocks = units.reshape(BLOCKS, ROWS_DEV, D)
    order_blocks = doc_order.reshape(BLOCKS, ROWS_DEV)
    offsets = list(range(-REACH, REACH + 1))

    def per_block(block):
        rows_units = unit_blocks[block]
        rows_order = order_blocks[block]
        row_best = jnp.full((ROWS_DEV,), -1.0, jnp.float32)
        col_parts = []
        for offset in offsets:
            other = ((block - offset) % BLOCKS).astype(jnp.int32)
            listed = jnp.logical_or(offset == 0, jnp.any(neighbours[block] == other))
            scores = jnp.dot(rows_units, unit_blocks[other].T, preferred_element_type=jnp.float32)
            valid = jnp.logical_and(order_blocks[other][None, :] < rows_order[:, None], listed)
            masked = jnp.where(valid, scores, jnp.float32(-1.0))
            row_best = jnp.maximum(row_best, lax.optimization_barrier(jnp.max(masked, axis=1)))
            col_parts.append(lax.optimization_barrier(jnp.max(masked, axis=0)))
        return (row_best, jnp.stack(col_parts))
    row_best, col_parts = lax.map(per_block, jnp.arange(BLOCKS, dtype=jnp.int32))
    later = jnp.full((BLOCKS, ROWS_DEV), -1.0, jnp.float32)
    for index, offset in enumerate(offsets):
        later = jnp.maximum(later, jnp.roll(col_parts[:, index], -offset, axis=0))
    return (row_best.reshape(DOCS), later.reshape(DOCS).astype(jnp.bfloat16))
```

```python
import functools

import jax
import jax.numpy as jnp
from jax import lax
from jax.experimental import pallas as pl
from jax.experimental.pallas import tpu as pltpu
from jax.sharding import PartitionSpec as P

MESH = pl.DeviceIdType.MESH
LANES = 128


def normalize(embeddings):
    values = embeddings.astype(jnp.float32)
    inverse = lax.rsqrt(jnp.sum(values * values, axis=-1, keepdims=True) + 1e-06)
    return (values * inverse).astype(jnp.bfloat16)


def kernel(blocks, chunk, emb_ref, order_ref, list_ref, out_ref, unit, unit_t, partner, partner_t,
           visit, order_v, order_p, spread, own_acc, par_acc, vis_acc, par_in, vis_in,
           send_sem, recv_sem, small_send, small_recv):
    rows = emb_ref.shape[0]
    chunks = rows // chunk
    group = lax.axis_index("groups")
    me = lax.axis_index("blk")
    odd = lax.rem(me, 2)
    mate = me + 1 - 2 * odd
    above = lax.rem(me + 2, blocks)
    below = lax.rem(me + blocks - 2, blocks)
    target = jnp.where(odd == 1, above, below)
    source = jnp.where(odd == 1, below, above)

    barrier = pltpu.get_barrier_semaphore()
    for peer in (mate, above, below):
        pl.semaphore_signal(barrier, inc=1, device_id=(group, peer), device_id_type=MESH)

    for c in range(chunks):
        part = pl.ds(c * chunk, chunk)
        unit[part, :] = normalize(emb_ref[part, :])

    pl.semaphore_wait(barrier, 3)

    def remote(src, dst, send, recv, peer):
        return pltpu.make_async_remote_copy(
            src_ref=src, dst_ref=dst, send_sem=send, recv_sem=recv,
            device_id=(group, peer), device_id_type=MESH,
        )

    order_copies = [
        remote(order_ref, order_v, small_send.at[0], small_recv.at[0], target),
        remote(order_ref, order_p, small_send.at[1], small_recv.at[1], mate),
    ]
    block_copies = []
    for c in range(chunks):
        part = pl.ds(c * chunk, chunk)
        block_copies.append(
            remote(unit.at[part], visit.at[part], send_sem.at[c], recv_sem.at[c], target)
        )
    mate_copy = remote(unit, partner, send_sem.at[chunks], recv_sem.at[chunks], mate)
    order_copies[0].start()
    block_copies[0].start()
    order_copies[1].start()
    mate_copy.start()
    for copy in block_copies[1:]:
        copy.start()

    low = jnp.float32(-1.0)

    def listed(block, entry):
        line = list_ref[pl.ds(block, 1), :]
        return jnp.max(jnp.where(line == entry, 1, 0), axis=1, keepdims=True) > 0

    def spread_order(ref):
        spread[...] = jnp.transpose(jnp.broadcast_to(ref[...], (LANES, rows)))

    def pair(left, left_part, right_t, right_order):
        scores = jnp.dot(left, right_t, preferred_element_type=jnp.float32)
        left_order = spread[left_part, :]
        ups, downs, wide_up, wide_down = [], [], None, None
        for g in range(rows // LANES):
            lanes = slice(g * LANES, (g + 1) * LANES)
            tile = scores[:, lanes]
            other = right_order[:, lanes]
            up = jnp.where(left_order < other, tile, low)
            down = jnp.where(left_order > other, tile, low)
            ups.append(jnp.max(up, axis=0, keepdims=True))
            downs.append(jnp.max(down, axis=0, keepdims=True))
            wide_up = up if g == 0 else jnp.maximum(wide_up, up)
            wide_down = down if g == 0 else jnp.maximum(wide_down, down)
        return jnp.concatenate(ups, 1), jnp.concatenate(downs, 1), wide_up, wide_down

    def fold(ref, line, values):
        ref[line:line + 1, :] = jnp.maximum(ref[line:line + 1, :], values)

    def narrow(values):
        return jnp.max(jnp.transpose(values), axis=0, keepdims=True)

    for ref in (own_acc, par_acc, vis_acc):
        ref[...] = jnp.full(ref.shape, low)

    my_order = order_ref[...]
    unit_t[...] = jnp.transpose(unit[...])
    spread_order(order_ref)
    for c in range(chunks):
        part = pl.ds(c * chunk, chunk)
        up, down, _, _ = pair(unit[part, :], part, unit_t[...], my_order)
        fold(own_acc, 0, up)
        fold(own_acc, 1, down)

    order_copies[1].wait_recv()
    mate_copy.wait_recv()
    own_has_mate = listed(me, mate)
    mate_has_own = listed(mate, me)

    @pl.when(odd == 1)
    def _():
        spread_order(order_p)
        for c in range(chunks):
            part = pl.ds(c * chunk, chunk)
            up, down, wide_up, wide_down = pair(partner[part, :], part, unit_t[...], my_order)
            fold(own_acc, 0, jnp.where(own_has_mate, up, low))
            fold(own_acc, 1, jnp.where(mate_has_own, down, low))
            lanes = slice(c * chunk, (c + 1) * chunk)
            par_acc[1:2, lanes] = jnp.where(own_has_mate, narrow(wide_up), low)
            par_acc[0:1, lanes] = jnp.where(mate_has_own, narrow(wide_down), low)

    @pl.when(odd == 0)
    def _():
        partner_t[...] = jnp.transpose(partner[...])

    order_copies[0].wait_recv()
    spread_order(order_v)
    own_has_vis = listed(me, source)
    vis_has_own = listed(source, me)
    mate_has_vis = listed(mate, source)
    vis_has_mate = listed(source, mate)
    for c in range(chunks):
        part = pl.ds(c * chunk, chunk)
        lanes = slice(c * chunk, (c + 1) * chunk)
        block_copies[c].wait_recv()
        up, down, wide_up, wide_down = pair(visit[part, :], part, unit_t[...], my_order)
        fold(own_acc, 0, jnp.where(own_has_vis, up, low))
        fold(own_acc, 1, jnp.where(vis_has_own, down, low))
        vis_acc[1:2, lanes] = jnp.where(own_has_vis, narrow(wide_up), low)
        vis_acc[0:1, lanes] = jnp.where(vis_has_own, narrow(wide_down), low)

        @pl.when(odd == 0)
        def _():
            up, down, wide_up, wide_down = pair(visit[part, :], part, partner_t[...], order_p[...])
            fold(par_acc, 0, jnp.where(mate_has_vis, up, low))
            fold(par_acc, 1, jnp.where(vis_has_mate, down, low))
            vis_acc[1:2, lanes] = jnp.maximum(
                vis_acc[1:2, lanes], jnp.where(mate_has_vis, narrow(wide_up), low)
            )
            vis_acc[0:1, lanes] = jnp.maximum(
                vis_acc[0:1, lanes], jnp.where(vis_has_mate, narrow(wide_down), low)
            )

    back = [
        remote(vis_acc, vis_in, small_send.at[2], small_recv.at[2], source),
        remote(par_acc, par_in, small_send.at[3], small_recv.at[3], mate),
    ]
    for copy in back:
        copy.start()
    for copy in order_copies + block_copies + [mate_copy]:
        copy.wait_send()
    back[1].wait_recv()
    best = jnp.maximum(own_acc[...], par_in[...])
    back[0].wait_recv()
    out_ref[...] = jnp.maximum(best, vis_in[...])
    for copy in back:
        copy.wait_send()


def local(blocks, embeddings, doc_order, neighbours):
    rows, width = embeddings.shape
    chunk = LANES
    chunks = rows // chunk
    vmem = pl.BlockSpec(memory_space=pltpu.VMEM)
    block = pltpu.VMEM((rows, width), jnp.bfloat16)
    block_t = pltpu.VMEM((width, rows), jnp.bfloat16)
    line = pltpu.VMEM((1, rows), jnp.int32)
    best = pltpu.VMEM((2, rows), jnp.float32)
    out = pl.pallas_call(
        functools.partial(kernel, blocks, chunk),
        out_shape=jax.ShapeDtypeStruct((2, rows), jnp.float32),
        in_specs=[vmem] * 3,
        out_specs=vmem,
        scratch_shapes=[
            block, block_t, block, block_t, block, line, line,
            pltpu.VMEM((rows, LANES), jnp.int32),
            best, best, best, best, best,
            pltpu.SemaphoreType.DMA((chunks + 1,)),
            pltpu.SemaphoreType.DMA((chunks + 1,)),
            pltpu.SemaphoreType.DMA((4,)),
            pltpu.SemaphoreType.DMA((4,)),
        ],
        compiler_params=pltpu.CompilerParams(
            collective_id=0, has_side_effects=True, vmem_limit_bytes=32 * 1024 * 1024
        ),
    )(embeddings, doc_order.reshape(1, rows), neighbours)
    return out[0], out[1].astype(jnp.bfloat16)


def solution(mesh):
    placed = (P(("groups", "blk"), None), P(("groups", "blk")), P("groups", None))
    return jax.shard_map(
        functools.partial(local, mesh.shape["blk"]),
        mesh=mesh,
        in_specs=placed,
        out_specs=(P(("groups", "blk")), P(("groups", "blk"))),
        check_vma=False,
    )
```

```python
import functools

import jax
import jax.numpy as jnp
from jax import lax
from jax.experimental import pallas as pl
from jax.experimental.pallas import tpu as pltpu
from jax.sharding import PartitionSpec as P

MESH = pl.DeviceIdType.MESH
LANES = 128


def normalize(embeddings):
    values = embeddings.astype(jnp.float32)
    inverse = lax.rsqrt(jnp.sum(values * values, axis=-1, keepdims=True) + 1e-06)
    return (values * inverse).astype(jnp.bfloat16)


def kernel(blocks, chunk, emb_hbm, order_hbm, list_hbm, out_ref, emb_ref, order_ref, list_ref,
           fetch_sem, unit, unit_t, partner, partner_t, visit, order_v, order_p, spread, own_acc, par_acc, vis_acc, par_in, vis_in,
           send_sem, recv_sem, small_send, small_recv):
    rows = emb_ref.shape[0]
    chunks = rows // chunk
    group = lax.axis_index("groups")
    me = lax.axis_index("blk")
    odd = lax.rem(me, 2)
    mate = me + 1 - 2 * odd
    above = lax.rem(me + 2, blocks)
    below = lax.rem(me + blocks - 2, blocks)
    target = jnp.where(odd == 1, above, below)
    source = jnp.where(odd == 1, below, above)

    fetches = [
        pltpu.make_async_copy(src, dst, fetch_sem.at[i])
        for i, (src, dst) in enumerate(
            ((emb_hbm, emb_ref), (order_hbm, order_ref), (list_hbm, list_ref))
        )
    ]
    for fetch in fetches:
        fetch.start()

    barrier = pltpu.get_barrier_semaphore()
    for peer in (mate, above, below):
        pl.semaphore_signal(barrier, inc=1, device_id=(group, peer), device_id_type=MESH)

    fetches[0].wait()
    for c in range(chunks):
        part = pl.ds(c * chunk, chunk)
        unit[part, :] = normalize(emb_ref[part, :])

    fetches[1].wait()
    fetches[2].wait()
    pl.semaphore_wait(barrier, 3)

    def remote(src, dst, send, recv, peer):
        return pltpu.make_async_remote_copy(
            src_ref=src, dst_ref=dst, send_sem=send, recv_sem=recv,
            device_id=(group, peer), device_id_type=MESH,
        )

    order_copies = [
        remote(order_ref, order_v, small_send.at[0], small_recv.at[0], target),
        remote(order_ref, order_p, small_send.at[1], small_recv.at[1], mate),
    ]
    block_copies = []
    for c in range(chunks):
        part = pl.ds(c * chunk, chunk)
        block_copies.append(
            remote(unit.at[part], visit.at[part], send_sem.at[c], recv_sem.at[c], target)
        )
    mate_copy = remote(unit, partner, send_sem.at[chunks], recv_sem.at[chunks], mate)
    order_copies[0].start()
    block_copies[0].start()
    order_copies[1].start()
    mate_copy.start()
    for copy in block_copies[1:]:
        copy.start()

    low = jnp.float32(-1.0)

    def listed(block, entry):
        lists = list_ref[...]
        here = jnp.logical_and(lax.broadcasted_iota(jnp.int32, lists.shape, 1) == block, lists == entry)
        return jnp.max(jnp.where(here, 1, 0), keepdims=True) > 0

    def spread_order(ref):
        spread[...] = jnp.transpose(jnp.broadcast_to(ref[...], (LANES, rows)))

    def pair(left, left_part, right_t, right_order):
        scores = jnp.dot(left, right_t, preferred_element_type=jnp.float32)
        left_order = spread[left_part, :]
        ups, downs, wide_up, wide_down = [], [], None, None
        for g in range(rows // LANES):
            lanes = slice(g * LANES, (g + 1) * LANES)
            tile = scores[:, lanes]
            other = right_order[:, lanes]
            up = jnp.where(left_order < other, tile, low)
            down = jnp.where(left_order > other, tile, low)
            ups.append(jnp.max(up, axis=0, keepdims=True))
            downs.append(jnp.max(down, axis=0, keepdims=True))
            wide_up = up if g == 0 else jnp.maximum(wide_up, up)
            wide_down = down if g == 0 else jnp.maximum(wide_down, down)
        return jnp.concatenate(ups, 1), jnp.concatenate(downs, 1), wide_up, wide_down

    def fold(ref, line, values):
        ref[line:line + 1, :] = jnp.maximum(ref[line:line + 1, :], values)

    def narrow(values):
        return jnp.max(jnp.transpose(values), axis=0, keepdims=True)

    for ref in (own_acc, par_acc, vis_acc):
        ref[...] = jnp.full(ref.shape, low)

    my_order = order_ref[...]
    unit_t[...] = jnp.transpose(unit[...])
    spread_order(order_ref)
    for c in range(chunks):
        part = pl.ds(c * chunk, chunk)
        up, down, _, _ = pair(unit[part, :], part, unit_t[...], my_order)
        fold(own_acc, 0, up)
        fold(own_acc, 1, down)

    order_copies[1].wait_recv()
    mate_copy.wait_recv()
    own_has_mate = listed(me, mate)
    mate_has_own = listed(mate, me)

    @pl.when(odd == 1)
    def _():
        spread_order(order_p)
        for c in range(chunks):
            part = pl.ds(c * chunk, chunk)
            up, down, wide_up, wide_down = pair(partner[part, :], part, unit_t[...], my_order)
            fold(own_acc, 0, jnp.where(own_has_mate, up, low))
            fold(own_acc, 1, jnp.where(mate_has_own, down, low))
            lanes = slice(c * chunk, (c + 1) * chunk)
            par_acc[1:2, lanes] = jnp.where(own_has_mate, narrow(wide_up), low)
            par_acc[0:1, lanes] = jnp.where(mate_has_own, narrow(wide_down), low)

    @pl.when(odd == 0)
    def _():
        partner_t[...] = jnp.transpose(partner[...])

    order_copies[0].wait_recv()
    spread_order(order_v)
    own_has_vis = listed(me, source)
    vis_has_own = listed(source, me)
    mate_has_vis = listed(mate, source)
    vis_has_mate = listed(source, mate)
    for c in range(chunks):
        part = pl.ds(c * chunk, chunk)
        lanes = slice(c * chunk, (c + 1) * chunk)
        block_copies[c].wait_recv()
        up, down, wide_up, wide_down = pair(visit[part, :], part, unit_t[...], my_order)
        fold(own_acc, 0, jnp.where(own_has_vis, up, low))
        fold(own_acc, 1, jnp.where(vis_has_own, down, low))
        vis_acc[1:2, lanes] = jnp.where(own_has_vis, narrow(wide_up), low)
        vis_acc[0:1, lanes] = jnp.where(vis_has_own, narrow(wide_down), low)

        @pl.when(odd == 0)
        def _():
            up, down, wide_up, wide_down = pair(visit[part, :], part, partner_t[...], order_p[...])
            fold(par_acc, 0, jnp.where(mate_has_vis, up, low))
            fold(par_acc, 1, jnp.where(vis_has_mate, down, low))
            vis_acc[1:2, lanes] = jnp.maximum(
                vis_acc[1:2, lanes], jnp.where(mate_has_vis, narrow(wide_up), low)
            )
            vis_acc[0:1, lanes] = jnp.maximum(
                vis_acc[0:1, lanes], jnp.where(vis_has_mate, narrow(wide_down), low)
            )

    back = [
        remote(vis_acc, vis_in, small_send.at[2], small_recv.at[2], source),
        remote(par_acc, par_in, small_send.at[3], small_recv.at[3], mate),
    ]
    for copy in back:
        copy.start()
    for copy in order_copies + block_copies + [mate_copy]:
        copy.wait_send()
    back[1].wait_recv()
    best = jnp.maximum(own_acc[...], par_in[...])
    back[0].wait_recv()
    out_ref[...] = jnp.maximum(best, vis_in[...])
    for copy in back:
        copy.wait_send()


def finish(best_ref, earlier_ref, later_ref):
    earlier_ref[...] = best_ref[0, :]
    later_ref[...] = best_ref[1, :].astype(jnp.bfloat16)


def local(blocks, embeddings, doc_order, neighbours):
    rows, width = embeddings.shape
    chunk = LANES
    chunks = rows // chunk
    vmem = pl.BlockSpec(memory_space=pltpu.VMEM)
    block = pltpu.VMEM((rows, width), jnp.bfloat16)
    block_t = pltpu.VMEM((width, rows), jnp.bfloat16)
    line = pltpu.VMEM((1, rows), jnp.int32)
    best = pltpu.VMEM((2, rows), jnp.float32)
    out = pl.pallas_call(
        functools.partial(kernel, blocks, chunk),
        out_shape=jax.ShapeDtypeStruct((2, rows), jnp.float32),
        in_specs=[pl.BlockSpec(memory_space=pltpu.HBM)] * 3,
        out_specs=vmem,
        scratch_shapes=[
            block, line, pltpu.VMEM(neighbours.shape[::-1], jnp.int32),
            pltpu.SemaphoreType.DMA((3,)),
            block, block_t, block, block_t, block, line, line,
            pltpu.VMEM((rows, LANES), jnp.int32),
            best, best, best, best, best,
            pltpu.SemaphoreType.DMA((chunks + 1,)),
            pltpu.SemaphoreType.DMA((chunks + 1,)),
            pltpu.SemaphoreType.DMA((4,)),
            pltpu.SemaphoreType.DMA((4,)),
        ],
        compiler_params=pltpu.CompilerParams(
            collective_id=0, has_side_effects=True, vmem_limit_bytes=60 * 1024 * 1024
        ),
    )(embeddings, doc_order.reshape(1, rows), neighbours.T)
    return pl.pallas_call(
        finish,
        out_shape=(
            jax.ShapeDtypeStruct((rows,), jnp.float32),
            jax.ShapeDtypeStruct((rows,), jnp.bfloat16),
        ),
        in_specs=[vmem],
        out_specs=(vmem, vmem),
        compiler_params=pltpu.CompilerParams(vmem_limit_bytes=60 * 1024 * 1024),
    )(out)


def solution(mesh):
    placed = (P(("groups", "blk"), None), P(("groups", "blk")), P("groups", None))
    return jax.shard_map(
        functools.partial(local, mesh.shape["blk"]),
        mesh=mesh,
        in_specs=placed,
        out_specs=(P(("groups", "blk")), P(("groups", "blk"))),
        check_vma=False,
    )
```

```python
import functools

import jax
import jax.numpy as jnp
from jax import lax
from jax.experimental import pallas as pl
from jax.experimental.pallas import tpu as pltpu
from jax.sharding import PartitionSpec as P

MESH = pl.DeviceIdType.MESH
LANES = 128


def normalize(embeddings):
    values = embeddings.astype(jnp.float32)
    inverse = lax.rsqrt(jnp.sum(values * values, axis=-1, keepdims=True) + 1e-06)
    return (values * inverse).astype(jnp.bfloat16)


def kernel(blocks, chunk, emb_hbm, order_hbm, list_hbm, out_ref, emb_ref, order_ref, list_ref,
           fetch_sem, unit, unit_t, partner, partner_t, visit, order_v, order_p, spread, own_acc, par_acc, vis_acc, par_in, vis_in,
           send_sem, recv_sem, small_send, small_recv):
    rows = emb_ref.shape[0]
    chunks = rows // chunk
    group = lax.axis_index("groups")
    me = lax.axis_index("blk")
    odd = lax.rem(me, 2)
    mate = me + 1 - 2 * odd
    above = lax.rem(me + 2, blocks)
    below = lax.rem(me + blocks - 2, blocks)
    target = jnp.where(odd == 1, above, below)
    source = jnp.where(odd == 1, below, above)

    fetches = [
        pltpu.make_async_copy(src, dst, fetch_sem.at[i])
        for i, (src, dst) in enumerate(
            [(order_hbm, order_ref), (list_hbm, list_ref)]
            + [(emb_hbm.at[pl.ds(c * chunk, chunk)], emb_ref.at[pl.ds(c * chunk, chunk)])
               for c in range(chunks)]
        )
    ]
    for i in [2, 0, 1] + list(range(3, 2 + chunks)):
        fetches[i].start()

    barrier = pltpu.get_barrier_semaphore()
    for peer in (mate, above, below):
        pl.semaphore_signal(barrier, inc=1, device_id=(group, peer), device_id_type=MESH)

    def make_unit(c):
        part = pl.ds(c * chunk, chunk)
        fetches[2 + c].wait()
        unit[part, :] = normalize(emb_ref[part, :])

    make_unit(0)
    fetches[0].wait()
    pl.semaphore_wait(barrier, 3)

    def remote(src, dst, send, recv, peer):
        return pltpu.make_async_remote_copy(
            src_ref=src, dst_ref=dst, send_sem=send, recv_sem=recv,
            device_id=(group, peer), device_id_type=MESH,
        )

    order_copies = [
        remote(order_ref, order_v, small_send.at[0], small_recv.at[0], target),
        remote(order_ref, order_p, small_send.at[1], small_recv.at[1], mate),
    ]
    block_copies = []
    for c in range(chunks):
        part = pl.ds(c * chunk, chunk)
        block_copies.append(
            remote(unit.at[part], visit.at[part], send_sem.at[c], recv_sem.at[c], target)
        )
    mate_copy = remote(unit, partner, send_sem.at[chunks], recv_sem.at[chunks], mate)
    order_copies[0].start()
    block_copies[0].start()
    for c in range(1, chunks):
        make_unit(c)
        block_copies[c].start()
    order_copies[1].start()
    mate_copy.start()
    fetches[1].wait()

    low = jnp.float32(-1.0)

    def listed(block, entry):
        lists = list_ref[...]
        here = jnp.logical_and(lax.broadcasted_iota(jnp.int32, lists.shape, 1) == block, lists == entry)
        return jnp.max(jnp.where(here, 1, 0), keepdims=True) > 0

    def spread_order(ref):
        spread[...] = jnp.transpose(jnp.broadcast_to(ref[...], (LANES, rows)))

    def pair(left, left_part, right_t, right_order):
        scores = jnp.dot(left, right_t, preferred_element_type=jnp.float32)
        left_order = spread[left_part, :]
        ups, downs, wide_up, wide_down = [], [], None, None
        for g in range(rows // LANES):
            lanes = slice(g * LANES, (g + 1) * LANES)
            tile = scores[:, lanes]
            other = right_order[:, lanes]
            up = jnp.where(left_order < other, tile, low)
            down = jnp.where(left_order > other, tile, low)
            ups.append(jnp.max(up, axis=0, keepdims=True))
            downs.append(jnp.max(down, axis=0, keepdims=True))
            wide_up = up if g == 0 else jnp.maximum(wide_up, up)
            wide_down = down if g == 0 else jnp.maximum(wide_down, down)
        return jnp.concatenate(ups, 1), jnp.concatenate(downs, 1), wide_up, wide_down

    def fold(ref, line, values):
        ref[line:line + 1, :] = jnp.maximum(ref[line:line + 1, :], values)

    def narrow(values):
        return jnp.max(jnp.transpose(values), axis=0, keepdims=True)

    for ref in (own_acc, par_acc, vis_acc):
        ref[...] = jnp.full(ref.shape, low)

    my_order = order_ref[...]
    unit_t[...] = jnp.transpose(unit[...])
    spread_order(order_ref)
    for c in range(chunks):
        part = pl.ds(c * chunk, chunk)
        up, down, _, _ = pair(unit[part, :], part, unit_t[...], my_order)
        fold(own_acc, 0, up)
        fold(own_acc, 1, down)

    order_copies[1].wait_recv()
    mate_copy.wait_recv()
    own_has_mate = listed(me, mate)
    mate_has_own = listed(mate, me)

    @pl.when(odd == 1)
    def _():
        spread_order(order_p)
        for c in range(chunks):
            part = pl.ds(c * chunk, chunk)
            up, down, wide_up, wide_down = pair(partner[part, :], part, unit_t[...], my_order)
            fold(own_acc, 0, jnp.where(own_has_mate, up, low))
            fold(own_acc, 1, jnp.where(mate_has_own, down, low))
            lanes = slice(c * chunk, (c + 1) * chunk)
            par_acc[1:2, lanes] = jnp.where(own_has_mate, narrow(wide_up), low)
            par_acc[0:1, lanes] = jnp.where(mate_has_own, narrow(wide_down), low)

    @pl.when(odd == 0)
    def _():
        partner_t[...] = jnp.transpose(partner[...])

    order_copies[0].wait_recv()
    spread_order(order_v)
    own_has_vis = listed(me, source)
    vis_has_own = listed(source, me)
    mate_has_vis = listed(mate, source)
    vis_has_mate = listed(source, mate)
    for c in range(chunks):
        part = pl.ds(c * chunk, chunk)
        lanes = slice(c * chunk, (c + 1) * chunk)
        block_copies[c].wait_recv()
        up, down, wide_up, wide_down = pair(visit[part, :], part, unit_t[...], my_order)
        fold(own_acc, 0, jnp.where(own_has_vis, up, low))
        fold(own_acc, 1, jnp.where(vis_has_own, down, low))
        vis_acc[1:2, lanes] = jnp.where(own_has_vis, narrow(wide_up), low)
        vis_acc[0:1, lanes] = jnp.where(vis_has_own, narrow(wide_down), low)

        @pl.when(odd == 0)
        def _():
            up, down, wide_up, wide_down = pair(visit[part, :], part, partner_t[...], order_p[...])
            fold(par_acc, 0, jnp.where(mate_has_vis, up, low))
            fold(par_acc, 1, jnp.where(vis_has_mate, down, low))
            vis_acc[1:2, lanes] = jnp.maximum(
                vis_acc[1:2, lanes], jnp.where(mate_has_vis, narrow(wide_up), low)
            )
            vis_acc[0:1, lanes] = jnp.maximum(
                vis_acc[0:1, lanes], jnp.where(vis_has_mate, narrow(wide_down), low)
            )

    back = [
        remote(vis_acc, vis_in, small_send.at[2], small_recv.at[2], source),
        remote(par_acc, par_in, small_send.at[3], small_recv.at[3], mate),
    ]
    for copy in back:
        copy.start()
    for copy in order_copies + block_copies + [mate_copy]:
        copy.wait_send()
    back[1].wait_recv()
    best = jnp.maximum(own_acc[...], par_in[...])
    back[0].wait_recv()
    out_ref[...] = jnp.maximum(best, vis_in[...])
    for copy in back:
        copy.wait_send()


def finish(best_ref, earlier_ref, later_ref):
    earlier_ref[...] = best_ref[0, :]
    later_ref[...] = best_ref[1, :].astype(jnp.bfloat16)


def local(blocks, embeddings, doc_order, neighbours):
    rows, width = embeddings.shape
    chunk = LANES
    chunks = rows // chunk
    vmem = pl.BlockSpec(memory_space=pltpu.VMEM)
    block = pltpu.VMEM((rows, width), jnp.bfloat16)
    block_t = pltpu.VMEM((width, rows), jnp.bfloat16)
    line = pltpu.VMEM((1, rows), jnp.int32)
    best = pltpu.VMEM((2, rows), jnp.float32)
    out = pl.pallas_call(
        functools.partial(kernel, blocks, chunk),
        out_shape=jax.ShapeDtypeStruct((2, rows), jnp.float32),
        in_specs=[pl.BlockSpec(memory_space=pltpu.HBM)] * 3,
        out_specs=vmem,
        scratch_shapes=[
            block, line, pltpu.VMEM(neighbours.shape[::-1], jnp.int32),
            pltpu.SemaphoreType.DMA((chunks + 2,)),
            block, block_t, block, block_t, block, line, line,
            pltpu.VMEM((rows, LANES), jnp.int32),
            best, best, best, best, best,
            pltpu.SemaphoreType.DMA((chunks + 1,)),
            pltpu.SemaphoreType.DMA((chunks + 1,)),
            pltpu.SemaphoreType.DMA((4,)),
            pltpu.SemaphoreType.DMA((4,)),
        ],
        compiler_params=pltpu.CompilerParams(
            collective_id=0, has_side_effects=True, vmem_limit_bytes=60 * 1024 * 1024
        ),
    )(embeddings, doc_order.reshape(1, rows), neighbours.T)
    return pl.pallas_call(
        finish,
        out_shape=(
            jax.ShapeDtypeStruct((rows,), jnp.float32),
            jax.ShapeDtypeStruct((rows,), jnp.bfloat16),
        ),
        in_specs=[vmem],
        out_specs=(vmem, vmem),
        compiler_params=pltpu.CompilerParams(vmem_limit_bytes=60 * 1024 * 1024),
    )(out)


def solution(mesh):
    placed = (P(("groups", "blk"), None), P(("groups", "blk")), P("groups", None))
    return jax.shard_map(
        functools.partial(local, mesh.shape["blk"]),
        mesh=mesh,
        in_specs=placed,
        out_specs=(P(("groups", "blk")), P(("groups", "blk"))),
        check_vma=False,
    )
```

```python
import functools

import jax
import jax.numpy as jnp
from jax import lax
from jax.experimental import pallas as pl
from jax.experimental.pallas import tpu as pltpu
from jax.sharding import PartitionSpec as P

MESH = pl.DeviceIdType.MESH
LANES = 128


def normalize(embeddings):
    values = embeddings.astype(jnp.float32)
    inverse = lax.rsqrt(jnp.sum(values * values, axis=-1, keepdims=True) + 1e-06)
    return (values * inverse).astype(jnp.bfloat16)


def kernel(blocks, chunk, emb_hbm, order_hbm, list_hbm, out_ref, emb_ref, order_ref, list_ref,
           fetch_sem, unit, unit_t, partner, partner_t, visit, order_v, order_p, spread, own_acc, par_acc, vis_acc, par_in, vis_in,
           send_sem, recv_sem, small_send, small_recv):
    rows = emb_ref.shape[0]
    chunks = rows // chunk
    group = lax.axis_index("groups")
    me = lax.axis_index("blk")
    odd = lax.rem(me, 2)
    mate = me + 1 - 2 * odd
    above = lax.rem(me + 2, blocks)
    below = lax.rem(me + blocks - 2, blocks)
    target = jnp.where(odd == 1, above, below)
    source = jnp.where(odd == 1, below, above)

    fetches = [
        pltpu.make_async_copy(src, dst, fetch_sem.at[i])
        for i, (src, dst) in enumerate(
            ((emb_hbm, emb_ref), (order_hbm, order_ref), (list_hbm, list_ref))
        )
    ]
    for fetch in fetches:
        fetch.start()

    barrier = pltpu.get_barrier_semaphore()
    for peer in (mate, above, below):
        pl.semaphore_signal(barrier, inc=1, device_id=(group, peer), device_id_type=MESH)

    fetches[0].wait()
    for c in range(chunks):
        part = pl.ds(c * chunk, chunk)
        unit[part, :] = normalize(emb_ref[part, :])

    fetches[1].wait()
    fetches[2].wait()
    pl.semaphore_wait(barrier, 3)

    def remote(src, dst, send, recv, peer):
        return pltpu.make_async_remote_copy(
            src_ref=src, dst_ref=dst, send_sem=send, recv_sem=recv,
            device_id=(group, peer), device_id_type=MESH,
        )

    order_copies = [
        remote(order_ref, order_v, small_send.at[0], small_recv.at[0], target),
        remote(order_ref, order_p, small_send.at[1], small_recv.at[1], mate),
    ]
    block_copies = []
    for c in range(chunks):
        part = pl.ds(c * chunk, chunk)
        block_copies.append(
            remote(unit.at[part], visit.at[part], send_sem.at[c], recv_sem.at[c], target)
        )
    mate_copy = remote(unit, partner, send_sem.at[chunks], recv_sem.at[chunks], mate)
    order_copies[0].start()
    block_copies[0].start()
    order_copies[1].start()
    mate_copy.start()
    for copy in block_copies[1:]:
        copy.start()

    low = jnp.float32(-1.0)

    def listed(block, entry):
        lists = list_ref[...]
        here = jnp.logical_and(lax.broadcasted_iota(jnp.int32, lists.shape, 1) == block, lists == entry)
        return jnp.max(jnp.where(here, 1, 0), keepdims=True) > 0

    def spread_order(ref):
        spread[...] = jnp.transpose(jnp.broadcast_to(ref[...], (LANES, rows)))

    def pair(left, left_part, right_t, right_order):
        scores = jnp.dot(left, right_t, preferred_element_type=jnp.float32)
        left_order = spread[left_part, :]
        ups, downs, wide_up, wide_down = [], [], None, None
        for g in range(rows // LANES):
            lanes = slice(g * LANES, (g + 1) * LANES)
            tile = scores[:, lanes]
            other = right_order[:, lanes]
            up = jnp.where(left_order < other, tile, low)
            down = jnp.where(left_order > other, tile, low)
            ups.append(jnp.max(up, axis=0, keepdims=True))
            downs.append(jnp.max(down, axis=0, keepdims=True))
            wide_up = up if g == 0 else jnp.maximum(wide_up, up)
            wide_down = down if g == 0 else jnp.maximum(wide_down, down)
        return jnp.concatenate(ups, 1), jnp.concatenate(downs, 1), wide_up, wide_down

    def fold(ref, line, values):
        ref[line:line + 1, :] = jnp.maximum(ref[line:line + 1, :], values)

    def narrow(values):
        return jnp.max(jnp.transpose(values), axis=0, keepdims=True)

    for ref in (own_acc, par_acc, vis_acc):
        ref[...] = jnp.full(ref.shape, low)

    my_order = order_ref[...]
    unit_t[...] = jnp.transpose(unit[...])
    spread_order(order_ref)
    for c in range(chunks):
        part = pl.ds(c * chunk, chunk)
        up, down, _, _ = pair(unit[part, :], part, unit_t[...], my_order)
        fold(own_acc, 0, up)
        fold(own_acc, 1, down)

    order_copies[1].wait_recv()
    mate_copy.wait_recv()
    own_has_mate = listed(me, mate)
    mate_has_own = listed(mate, me)

    @pl.when(odd == 1)
    def _():
        spread_order(order_p)
        for c in range(chunks):
            part = pl.ds(c * chunk, chunk)
            up, down, wide_up, wide_down = pair(partner[part, :], part, unit_t[...], my_order)
            fold(own_acc, 0, jnp.where(own_has_mate, up, low))
            fold(own_acc, 1, jnp.where(mate_has_own, down, low))
            lanes = slice(c * chunk, (c + 1) * chunk)
            par_acc[1:2, lanes] = jnp.where(own_has_mate, narrow(wide_up), low)
            par_acc[0:1, lanes] = jnp.where(mate_has_own, narrow(wide_down), low)

    @pl.when(odd == 0)
    def _():
        partner_t[...] = jnp.transpose(partner[...])

    order_copies[0].wait_recv()
    spread_order(order_v)
    own_has_vis = listed(me, source)
    vis_has_own = listed(source, me)
    mate_has_vis = listed(mate, source)
    vis_has_mate = listed(source, mate)
    for c in range(chunks):
        part = pl.ds(c * chunk, chunk)
        lanes = slice(c * chunk, (c + 1) * chunk)
        block_copies[c].wait_recv()
        up, down, wide_up, wide_down = pair(visit[part, :], part, unit_t[...], my_order)
        fold(own_acc, 0, jnp.where(own_has_vis, up, low))
        fold(own_acc, 1, jnp.where(vis_has_own, down, low))
        vis_acc[1:2, lanes] = jnp.where(own_has_vis, narrow(wide_up), low)
        vis_acc[0:1, lanes] = jnp.where(vis_has_own, narrow(wide_down), low)

        @pl.when(odd == 0)
        def _():
            up, down, wide_up, wide_down = pair(visit[part, :], part, partner_t[...], order_p[...])
            fold(par_acc, 0, jnp.where(mate_has_vis, up, low))
            fold(par_acc, 1, jnp.where(vis_has_mate, down, low))
            vis_acc[1:2, lanes] = jnp.maximum(
                vis_acc[1:2, lanes], jnp.where(mate_has_vis, narrow(wide_up), low)
            )
            vis_acc[0:1, lanes] = jnp.maximum(
                vis_acc[0:1, lanes], jnp.where(vis_has_mate, narrow(wide_down), low)
            )

    back = [
        remote(vis_acc, vis_in, small_send.at[2], small_recv.at[2], source),
        remote(par_acc, par_in, small_send.at[3], small_recv.at[3], mate),
    ]
    for copy in back:
        copy.start()
    for copy in order_copies + block_copies + [mate_copy]:
        copy.wait_send()
    back[1].wait_recv()
    best = jnp.maximum(own_acc[...], par_in[...])
    back[0].wait_recv()
    out_ref[...] = jnp.maximum(best, vis_in[...])
    for copy in back:
        copy.wait_send()


def finish(best_ref, earlier_ref, later_ref):
    earlier_ref[...] = best_ref[0, :]
    later_ref[...] = best_ref[1, :].astype(jnp.bfloat16)


def local(blocks, embeddings, doc_order, neighbours):
    rows, width = embeddings.shape
    chunk = LANES
    chunks = rows // chunk
    vmem = pl.BlockSpec(memory_space=pltpu.VMEM)
    block = pltpu.VMEM((rows, width), jnp.bfloat16)
    block_t = pltpu.VMEM((width, rows), jnp.bfloat16)
    line = pltpu.VMEM((1, rows), jnp.int32)
    best = pltpu.VMEM((2, rows), jnp.float32)
    out = pl.pallas_call(
        functools.partial(kernel, blocks, chunk),
        out_shape=pltpu.VMEM((2, rows), jnp.float32),
        in_specs=[pl.BlockSpec(memory_space=pltpu.HBM)] * 3,
        out_specs=vmem,
        scratch_shapes=[
            block, line, pltpu.VMEM(neighbours.shape[::-1], jnp.int32),
            pltpu.SemaphoreType.DMA((3,)),
            block, block_t, block, block_t, block, line, line,
            pltpu.VMEM((rows, LANES), jnp.int32),
            best, best, best, best, best,
            pltpu.SemaphoreType.DMA((chunks + 1,)),
            pltpu.SemaphoreType.DMA((chunks + 1,)),
            pltpu.SemaphoreType.DMA((4,)),
            pltpu.SemaphoreType.DMA((4,)),
        ],
        compiler_params=pltpu.CompilerParams(
            collective_id=0, has_side_effects=True, vmem_limit_bytes=60 * 1024 * 1024
        ),
    )(embeddings, doc_order.reshape(1, rows), neighbours.T)
    return pl.pallas_call(
        finish,
        out_shape=(
            jax.ShapeDtypeStruct((rows,), jnp.float32),
            jax.ShapeDtypeStruct((rows,), jnp.bfloat16),
        ),
        in_specs=[vmem],
        out_specs=(vmem, vmem),
        compiler_params=pltpu.CompilerParams(vmem_limit_bytes=1024 * 1024),
    )(out)


def solution(mesh):
    placed = (P(("groups", "blk"), None), P(("groups", "blk")), P("groups", None))
    return jax.shard_map(
        functools.partial(local, mesh.shape["blk"]),
        mesh=mesh,
        in_specs=placed,
        out_specs=(P(("groups", "blk")), P(("groups", "blk"))),
        check_vma=False,
    )
```

```python
import functools

import jax
import jax.numpy as jnp
from jax import lax
from jax.experimental import pallas as pl
from jax.experimental.pallas import tpu as pltpu
from jax.sharding import PartitionSpec as P

MESH = pl.DeviceIdType.MESH
LANES = 128


def normalize(embeddings):
    values = embeddings.astype(jnp.float32)
    inverse = lax.rsqrt(jnp.sum(values * values, axis=-1, keepdims=True) + 1e-06)
    return (values * inverse).astype(jnp.bfloat16)


def kernel(blocks, chunk, emb_hbm, order_hbm, list_hbm, out_ref, emb_ref, order_ref, list_ref,
           fetch_sem, unit, unit_t, partner, partner_t, visit, visit_unit, order_v, order_p, spread, own_acc, par_acc, vis_acc, par_in, vis_in,
           send_sem, recv_sem, small_send, small_recv):
    rows = emb_ref.shape[0]
    chunks = rows // chunk
    group = lax.axis_index("groups")
    me = lax.axis_index("blk")
    odd = lax.rem(me, 2)
    mate = me + 1 - 2 * odd
    above = lax.rem(me + 2, blocks)
    below = lax.rem(me + blocks - 2, blocks)
    target = jnp.where(odd == 1, above, below)
    source = jnp.where(odd == 1, below, above)

    fetches = [
        pltpu.make_async_copy(src, dst, fetch_sem.at[i])
        for i, (src, dst) in enumerate(
            ((emb_hbm, emb_ref), (order_hbm, order_ref), (list_hbm, list_ref))
        )
    ]
    for fetch in fetches:
        fetch.start()

    barrier = pltpu.get_barrier_semaphore()
    for peer in (mate, above, below):
        pl.semaphore_signal(barrier, inc=1, device_id=(group, peer), device_id_type=MESH)

    fetches[1].wait()
    pl.semaphore_wait(barrier, 3)

    def remote(src, dst, send, recv, peer):
        return pltpu.make_async_remote_copy(
            src_ref=src, dst_ref=dst, send_sem=send, recv_sem=recv,
            device_id=(group, peer), device_id_type=MESH,
        )

    order_copies = [
        remote(order_ref, order_v, small_send.at[0], small_recv.at[0], target),
        remote(order_ref, order_p, small_send.at[1], small_recv.at[1], mate),
    ]
    block_copies = []
    for c in range(chunks):
        part = pl.ds(c * chunk, chunk)
        block_copies.append(
            remote((unit if c else emb_hbm).at[part], visit.at[part], send_sem.at[c], recv_sem.at[c], target)
        )
    mate_copy = remote(unit, partner, send_sem.at[chunks], recv_sem.at[chunks], mate)
    order_copies[0].start()
    block_copies[0].start()
    fetches[0].wait()
    for c in range(chunks):
        part = pl.ds(c * chunk, chunk)
        unit[part, :] = normalize(emb_ref[part, :])
        if c:
            block_copies[c].start()
    order_copies[1].start()
    mate_copy.start()
    fetches[2].wait()

    low = jnp.float32(-1.0)

    def listed(block, entry):
        lists = list_ref[...]
        here = jnp.logical_and(lax.broadcasted_iota(jnp.int32, lists.shape, 1) == block, lists == entry)
        return jnp.max(jnp.where(here, 1, 0), keepdims=True) > 0

    def spread_order(ref):
        spread[...] = jnp.transpose(jnp.broadcast_to(ref[...], (LANES, rows)))

    def pair(left, left_part, right_t, right_order):
        scores = jnp.dot(left, right_t, preferred_element_type=jnp.float32)
        left_order = spread[left_part, :]
        ups, downs, wide_up, wide_down = [], [], None, None
        for g in range(rows // LANES):
            lanes = slice(g * LANES, (g + 1) * LANES)
            tile = scores[:, lanes]
            other = right_order[:, lanes]
            up = jnp.where(left_order < other, tile, low)
            down = jnp.where(left_order > other, tile, low)
            ups.append(jnp.max(up, axis=0, keepdims=True))
            downs.append(jnp.max(down, axis=0, keepdims=True))
            wide_up = up if g == 0 else jnp.maximum(wide_up, up)
            wide_down = down if g == 0 else jnp.maximum(wide_down, down)
        return jnp.concatenate(ups, 1), jnp.concatenate(downs, 1), wide_up, wide_down

    def fold(ref, line, values):
        ref[line:line + 1, :] = jnp.maximum(ref[line:line + 1, :], values)

    def narrow(values):
        return jnp.max(jnp.transpose(values), axis=0, keepdims=True)

    for ref in (own_acc, par_acc, vis_acc):
        ref[...] = jnp.full(ref.shape, low)

    my_order = order_ref[...]
    unit_t[...] = jnp.transpose(unit[...])
    spread_order(order_ref)
    for c in range(chunks):
        part = pl.ds(c * chunk, chunk)
        up, down, _, _ = pair(unit[part, :], part, unit_t[...], my_order)
        fold(own_acc, 0, up)
        fold(own_acc, 1, down)

    order_copies[1].wait_recv()
    mate_copy.wait_recv()
    own_has_mate = listed(me, mate)
    mate_has_own = listed(mate, me)

    @pl.when(odd == 1)
    def _():
        spread_order(order_p)
        for c in range(chunks):
            part = pl.ds(c * chunk, chunk)
            up, down, wide_up, wide_down = pair(partner[part, :], part, unit_t[...], my_order)
            fold(own_acc, 0, jnp.where(own_has_mate, up, low))
            fold(own_acc, 1, jnp.where(mate_has_own, down, low))
            lanes = slice(c * chunk, (c + 1) * chunk)
            par_acc[1:2, lanes] = jnp.where(own_has_mate, narrow(wide_up), low)
            par_acc[0:1, lanes] = jnp.where(mate_has_own, narrow(wide_down), low)

    @pl.when(odd == 0)
    def _():
        partner_t[...] = jnp.transpose(partner[...])

    order_copies[0].wait_recv()
    spread_order(order_v)
    own_has_vis = listed(me, source)
    vis_has_own = listed(source, me)
    mate_has_vis = listed(mate, source)
    vis_has_mate = listed(source, mate)
    for c in range(chunks):
        part = pl.ds(c * chunk, chunk)
        lanes = slice(c * chunk, (c + 1) * chunk)
        block_copies[c].wait_recv()
        visit_unit[part, :] = visit[part, :] if c else normalize(visit[part, :])
        up, down, wide_up, wide_down = pair(visit_unit[part, :], part, unit_t[...], my_order)
        fold(own_acc, 0, jnp.where(own_has_vis, up, low))
        fold(own_acc, 1, jnp.where(vis_has_own, down, low))
        vis_acc[1:2, lanes] = jnp.where(own_has_vis, narrow(wide_up), low)
        vis_acc[0:1, lanes] = jnp.where(vis_has_own, narrow(wide_down), low)

        @pl.when(odd == 0)
        def _():
            up, down, wide_up, wide_down = pair(visit_unit[part, :], part, partner_t[...], order_p[...])
            fold(par_acc, 0, jnp.where(mate_has_vis, up, low))
            fold(par_acc, 1, jnp.where(vis_has_mate, down, low))
            vis_acc[1:2, lanes] = jnp.maximum(
                vis_acc[1:2, lanes], jnp.where(mate_has_vis, narrow(wide_up), low)
            )
            vis_acc[0:1, lanes] = jnp.maximum(
                vis_acc[0:1, lanes], jnp.where(vis_has_mate, narrow(wide_down), low)
            )

    back = [
        remote(vis_acc, vis_in, small_send.at[2], small_recv.at[2], source),
        remote(par_acc, par_in, small_send.at[3], small_recv.at[3], mate),
    ]
    for copy in back:
        copy.start()
    for copy in order_copies + block_copies + [mate_copy]:
        copy.wait_send()
    back[1].wait_recv()
    best = jnp.maximum(own_acc[...], par_in[...])
    back[0].wait_recv()
    out_ref[...] = jnp.maximum(best, vis_in[...])
    for copy in back:
        copy.wait_send()


def finish(best_ref, earlier_ref, later_ref):
    earlier_ref[...] = best_ref[0, :]
    later_ref[...] = best_ref[1, :].astype(jnp.bfloat16)


def local(blocks, embeddings, doc_order, neighbours):
    rows, width = embeddings.shape
    chunk = LANES
    chunks = rows // chunk
    vmem = pl.BlockSpec(memory_space=pltpu.VMEM)
    block = pltpu.VMEM((rows, width), jnp.bfloat16)
    block_t = pltpu.VMEM((width, rows), jnp.bfloat16)
    line = pltpu.VMEM((1, rows), jnp.int32)
    best = pltpu.VMEM((2, rows), jnp.float32)
    out = pl.pallas_call(
        functools.partial(kernel, blocks, chunk),
        out_shape=pltpu.VMEM((2, rows), jnp.float32),
        in_specs=[pl.BlockSpec(memory_space=pltpu.HBM)] * 3,
        out_specs=vmem,
        scratch_shapes=[
            block, line, pltpu.VMEM(neighbours.shape[::-1], jnp.int32),
            pltpu.SemaphoreType.DMA((3,)),
            block, block_t, block, block_t, block, block, line, line,
            pltpu.VMEM((rows, LANES), jnp.int32),
            best, best, best, best, best,
            pltpu.SemaphoreType.DMA((chunks + 1,)),
            pltpu.SemaphoreType.DMA((chunks + 1,)),
            pltpu.SemaphoreType.DMA((4,)),
            pltpu.SemaphoreType.DMA((4,)),
        ],
        compiler_params=pltpu.CompilerParams(
            collective_id=0, has_side_effects=True, vmem_limit_bytes=60 * 1024 * 1024
        ),
    )(embeddings, doc_order.reshape(1, rows), neighbours.T)
    return pl.pallas_call(
        finish,
        out_shape=(
            jax.ShapeDtypeStruct((rows,), jnp.float32),
            jax.ShapeDtypeStruct((rows,), jnp.bfloat16),
        ),
        in_specs=[vmem],
        out_specs=(vmem, vmem),
        compiler_params=pltpu.CompilerParams(vmem_limit_bytes=1024 * 1024),
    )(out)


def solution(mesh):
    placed = (P(("groups", "blk"), None), P(("groups", "blk")), P("groups", None))
    return jax.shard_map(
        functools.partial(local, mesh.shape["blk"]),
        mesh=mesh,
        in_specs=placed,
        out_specs=(P(("groups", "blk")), P(("groups", "blk"))),
        check_vma=False,
    )
```
